32 devices in a mesh: pair: 8 (over z, x), virt: 4 (over y, core).
Axes of the slice: x: 2, y: 2, z: 4, core: 2. Of those that a mesh axis runs over, the one named last changes fastest.
Arguments:
- amplitudes: bfloat16 [2048, 3, 4096], P('pair'), may hold values from -6 to 6
- screen: int32 [2048, 3], P('pair'), may hold values from 0 to 15, all different within a row; in each aligned block of 256 rows (0 to 255, 256 to 511, ...) at most 96 rows name the same one
- integrals: bfloat16 [16, 4096, 8192], P('pair', None, 'virt'), may hold values from -0.0546875 to 0.0546875
- other: float32 [2048, 8192], P('pair', 'virt'), may hold values from -6 to 6
- occ_first: float32 [32], replicated, may hold values from -2 to -0.4
- occ_second: float32 [64], replicated, may hold values from -2 to -0.4
- virt_first: float32 [2, 64], replicated, may hold values from 0.3 to 3
- virt_second: float32 [2, 64], replicated, may hold values from 0.3 to 3
Outputs:
- new_amplitudes: float32 [2048, 8192], P('pair', 'virt')
The draws below stay inside these ranges and needn't reach their ends.
Inputs may be any that keep to these rules, and one draw needn't show every extreme that they name: `screen`: the 3 entries of a row differ. Within each aligned block of 256 rows (the rows of one pair index) no tile pair is named more than 96 times, and some tile pair is named exactly 96 times.
All inputs are finite; a program needn't handle non-finite values.
Results may differ from the reference program's by a relative error of at most 0.0003.
Values may be sent and summed in bfloat16 or wider, within the bound.
No kernel may reach another device: no remote copies, remote signals or barrier semaphores. Data moves between devices by JAX's collectives and lax.ppermute only.
A program may use at most 192 MiB of HBM per device.

```python
import math
import jax
import jax.numpy as jnp
import numpy as np
from jax import lax

TILE = 64
NAB = 2
TOP = 3
NJ = 64
PAIR_DEV = 256
PAIRS = 2048
NCD = 16
CD = 4096
AB = 8192
CAP = 96


def block_scale(stream_key, extent, shards, low, top_value):
    loudness = 1.0
    for dim, blocks in shards:
        heights = jax.random.uniform(jax.random.fold_in(jax.random.fold_in(stream_key, 6), dim), (blocks,), jnp.float32, low / len(shards), top_value / len(shards))
        loudness = loudness * jnp.repeat(jnp.exp(heights), extent[dim] // blocks).reshape((-1,) + (1,) * (len(extent) - 1 - dim))
    return loudness


def routed_block(key, own, number, rows, number_of, top, limit, slope):
    order = jax.random.permutation(key, number_of)
    crowded, ordinary = load_shares(number_of, rows * top, limit, slope, True), load_shares(number_of, rows * top, limit, slope, False)
    places = jnp.arange(number_of)

    def named(tallies, turn):
        used = int((tallies > 0).sum())
        fixed = max(1, used // 4)
        moved = fixed + (places - fixed + turn * (used - fixed)) % max(1, number_of - fixed)
        return jnp.zeros((number_of,), jnp.int32).at[order[jnp.where(places < fixed, places, moved)]].set(jnp.asarray(tallies, jnp.int32))

    tallies = jnp.where(number % 4 == 0, named(crowded, number // 4), named(ordinary, number - number // 4 - 1))
    mixed = jax.random.permutation(jax.random.fold_in(own, 3), number_of)
    source_of, taker = mixed[0:number_of // 2 * 2:2], mixed[1:number_of // 2 * 2:2]
    room = jnp.minimum(tallies[source_of] - 1, limit - tallies[taker]) // 2
    room = jnp.where((source_of == order[0]) | (taker == order[0]) | (tallies[taker] == 0), 0, jnp.maximum(room, 0))
    moved = jax.random.randint(jax.random.fold_in(own, 4), (number_of // 2,), 0, 1 << 20) % (room + 1)
    tallies = tallies.at[source_of].add(-moved).at[taker].add(moved)
    labels = jnp.searchsorted(jnp.cumsum(tallies), jnp.arange(rows * top), side="right").astype(jnp.int32)
    listing = labels.reshape(top, rows).T
    listing = listing[jax.random.permutation(jax.random.fold_in(own, 1), rows)]
    turn = jax.random.randint(jax.random.fold_in(own, 2), (rows, 1), 0, top)
    return jnp.take_along_axis(listing, (jnp.arange(top)[None, :] + turn) % top, axis=1)


def load_shares(number_of, total, most, slope, full):
    portions = [(1 << 20) // math.isqrt(standing ** slope) + 1 for standing in range(1, number_of + 1)]
    largest = most if full else min(most, max(-(-total // number_of), total * portions[0] // sum(portions)))
    least = 1 if total - largest >= number_of - 1 else 0
    given, rest = [largest] + [least] * (number_of - 1), total - largest - least * (number_of - 1)
    while rest > 0:
        free = [i for i in range(1, number_of) if given[i] < largest] or [i for i in range(1, number_of) if given[i] < most]
        pool, budget = sum([portions[i] for i in free]), rest
        for i in free:
            more = min(most - given[i], max(1, budget * portions[i] // pool), rest)
            given[i] = given[i] + more
            rest = rest - more
    return np.array(given)


def gaussian(stream_key, dims, deviation, reach, split=(), kind=jnp.bfloat16):
    drawn = deviation * jax.random.normal(stream_key, dims, jnp.float32)
    if split:
        drawn = drawn * block_scale(stream_key, dims, split, -0.22, 0.18)
    return jnp.clip(drawn, -reach, reach).astype(kind)


def setup_inputs(seed: int = 0) -> dict:
    splits = jax.random.split(jax.random.key(seed), 9)
    amplitudes = gaussian(splits[0], (PAIRS, TOP, CD), 1.0, 6.0, ((0, 8),))
    screen_keys = jax.random.split(jax.random.fold_in(splits[1], 1), PAIRS // PAIR_DEV)
    screen_turns = jax.random.permutation(jax.random.fold_in(splits[1], 3), PAIRS // PAIR_DEV)
    screen = jax.vmap(lambda own, number: routed_block(jax.random.fold_in(splits[1], 2), own, number, PAIR_DEV, NCD, TOP, CAP, 2))(screen_keys, screen_turns).reshape((PAIRS, TOP))
    integrals = gaussian(splits[2], (NCD, CD, AB), (CD * TOP) ** -0.5, 0.0546875, ((0, 8), (2, 4)))
    other = gaussian(splits[3], (PAIRS, AB), 1.0, 6.0, ((0, 8), (1, 4)), jnp.float32)
    occ_first = jnp.clip(jax.random.uniform(splits[4], (PAIRS // NJ,), jnp.float32, -2.0, -0.4), -2.0, -0.4)
    occ_second = jnp.clip(jax.random.uniform(splits[5], (NJ,), jnp.float32, -2.0, -0.4), -2.0, -0.4)
    virt_first = jnp.clip(jax.random.uniform(splits[6], (NAB, TILE), jnp.float32, 0.3, 3.0), 0.3, 3.0)
    virt_second = jnp.clip(jax.random.uniform(splits[7], (NAB, TILE), jnp.float32, 0.3, 3.0), 0.3, 3.0)
    return {"amplitudes": amplitudes, "screen": screen, "integrals": integrals, "other": other, "occ_first": occ_first, "occ_second": occ_second, "virt_first": virt_first, "virt_second": virt_second}


def reference(amplitudes, screen, integrals, other, occ_first, occ_second, virt_first, virt_second):
    pairs, top, width = amplitudes.shape
    experts = integrals.shape[0]
    blocks = pairs // PAIR_DEV
    flat = screen.reshape(blocks, PAIR_DEV * top)
    onehot = (flat[:, :, None] == jnp.arange(experts, dtype=jnp.int32)[None, None, :]).astype(jnp.int32)
    slots = jnp.sum((jnp.cumsum(onehot, axis=1) - 1) * onehot, axis=2).astype(jnp.int32)
    gslot = (slots + (jnp.arange(blocks, dtype=jnp.int32) * CAP)[:, None]).reshape(-1)
    rowid = (jnp.arange(pairs * top, dtype=jnp.int32) // top).astype(jnp.int32)
    eflat = flat.reshape(-1)
    buffer = jnp.zeros((experts, blocks * CAP, width), amplitudes.dtype)
    buffer = buffer.at[eflat, gslot].set(amplitudes.reshape(-1, width))
    owner = jnp.full((experts, blocks * CAP), pairs, jnp.int32).at[eflat, gslot].set(rowid)

    def add_expert(total, index):
        product = jnp.dot(buffer[index], integrals[index], preferred_element_type=jnp.float32)
        return total.at[owner[index]].add(product, mode="drop"), None

    ladder, unused = lax.scan(add_expert, jnp.zeros((pairs, AB), jnp.float32), jnp.arange(experts, dtype=jnp.int32))
    occ_sum = (occ_first[:, None] + occ_second[None, :]).reshape(pairs)
    virt_sum = (virt_first[:, :, None] + virt_second[:, None, :]).reshape(AB)
    denom = occ_sum[:, None] - virt_sum[None, :]
    return (0.5 * ladder + other) / denom
```

```python
import functools

import jax
import jax.numpy as jnp
from jax import lax
from jax.experimental import pallas as pl
from jax.experimental.pallas import tpu as pltpu
from jax.sharding import PartitionSpec as P

VMEM_LIMIT = 56 * 1024 * 1024
F32 = jnp.float32
BF16 = jnp.bfloat16
COL_CHUNKS = 2


def params():
    return pltpu.CompilerParams(vmem_limit_bytes=VMEM_LIMIT)


def cost(flops, nbytes):
    return pl.CostEstimate(flops=int(flops), bytes_accessed=int(nbytes), transcendentals=0)


def encode(v):
    w = v * 8.0
    sq = w * w
    quad = sq * sq
    return ((w * jnp.abs(w)) * (quad * sq)).astype(BF16)


def decode(code):
    c = code.astype(F32)
    a = jnp.abs(c)
    t = lax.rsqrt(jnp.maximum(a, 1e-37))
    u = lax.rsqrt(t)
    root = u * lax.rsqrt(u) * 0.125
    root = jnp.where(a < 1e-37, 0.0, root)
    return jnp.where(c < 0.0, -root, root)


def pack_kernel(code_ref, tiles_ref, out_ref):
    block = out_ref.shape[0]
    top, rows, _ = tiles_ref.shape
    want = lax.broadcasted_iota(jnp.int32, (block, rows), 0) + pl.program_id(0) * block
    total = None
    for k in range(top):
        pick = (want == code_ref[k : k + 1, :]).astype(F32).astype(BF16)
        part = jnp.dot(pick, tiles_ref[k], preferred_element_type=F32)
        total = part if total is None else total + part
    out_ref[...] = total.astype(BF16)


def pack(codes, tiles, n_slots):
    top, rows, width = tiles.shape
    steps = 4
    return pl.pallas_call(
        pack_kernel,
        grid=(steps,),
        in_specs=[
            pl.BlockSpec((top, rows), lambda i: (0, 0)),
            pl.BlockSpec((top, rows, width), lambda i: (0, 0, 0)),
        ],
        out_specs=pl.BlockSpec((n_slots // steps, width), lambda i: (i, 0)),
        out_shape=jax.ShapeDtypeStruct((n_slots, width), BF16),
        compiler_params=params(),
        cost_estimate=cost(2 * n_slots * top * rows * width, 4 * n_slots * width),
        name="pack_tiles",
    )(codes, tiles)


def product_kernel(cap, place_ref, *refs):
    *parts, w_ref, keep_ref, send_ref, acc_ref = refs
    quarter = parts[0].shape[1]
    total = None
    for j, lhs in enumerate(parts):
        q = lax.bitwise_xor(place_ref[0], j)
        rhs = w_ref[0, pl.ds(pl.multiple_of(q * quarter, quarter), quarter), :]
        part = jnp.dot(lhs[...], rhs, preferred_element_type=F32)
        total = part if total is None else total + part
    acc_ref[...] = total.reshape(acc_ref.shape)
    mine = place_ref[1]
    for g in range(acc_ref.shape[0] // 2):
        keep_ref[g] = acc_ref[2 * g + mine]
        send_ref[g] = encode(acc_ref[2 * g + 1 - mine])


def product(place, lhs, integrals, c, first, cols, cap):
    slots, quarter = lhs[0].shape
    width = integrals.shape[1]
    step = min(256, cols)
    sources = slots // cap
    half = sources // 2
    base = first // step
    return pl.pallas_call(
        functools.partial(product_kernel, cap),
        grid_spec=pltpu.PrefetchScalarGridSpec(
            num_scalar_prefetch=1,
            grid=(cols // step,),
            in_specs=[pl.BlockSpec((slots, quarter), lambda j, s: (0, 0))] * len(lhs)
            + [pl.BlockSpec((1, width, step), lambda j, s: (c, 0, base + j))],
            out_specs=[
                pl.BlockSpec((half, cap, step), lambda j, s: (0, 0, j)),
                pl.BlockSpec((half, cap, step), lambda j, s: (0, 0, j)),
            ],
            scratch_shapes=[pltpu.VMEM((sources, cap, step), F32)],
        ),
        out_shape=[
            jax.ShapeDtypeStruct((half, cap, cols), F32),
            jax.ShapeDtypeStruct((half, cap, cols), BF16),
        ],
        compiler_params=params(),
        cost_estimate=cost(2 * slots * width * cols, 2 * width * cols + 2 * slots * width + 4 * slots * cols),
        name="tile_products",
    )(place, *lhs, integrals)


def merge_kernel(place_ref, inv_ref, keep0, keep1, got0, got1, own_ref, send_ref):
    _, cap, _ = keep0.shape
    rows = inv_ref.shape[1]
    lane = lax.broadcasted_iota(jnp.int32, (rows, 4 * cap), 1)
    hit = None
    for c in range(4):
        slot = inv_ref[0, :, c : c + 1]
        one = lane == jnp.where(slot < 0, -1, slot + c * cap)
        hit = one if hit is None else hit | one
    pick = hit.astype(F32).astype(BF16)
    values = jnp.concatenate(
        [keep0[0], keep1[0], decode(got0[0]), decode(got1[0])], axis=0
    )
    high = values.astype(BF16)
    low = (values - high.astype(F32)).astype(BF16)
    dense = jnp.dot(pick, high, preferred_element_type=F32)
    dense = dense + jnp.dot(pick, low, preferred_element_type=F32)
    send_ref[0] = encode(dense)

    @pl.when(pl.program_id(1) == place_ref[2])
    def _():
        own_ref[...] = dense


def merge(place, inv, keep, got):
    groups, cap, cols = keep[0].shape
    rows = inv.shape[1]
    step = min(512, cols)
    spec = pl.BlockSpec((1, cap, step), lambda j, g, s: (g, 0, j))
    return pl.pallas_call(
        merge_kernel,
        grid_spec=pltpu.PrefetchScalarGridSpec(
            num_scalar_prefetch=1,
            grid=(cols // step, groups),
            in_specs=[pl.BlockSpec((1, rows, 4), lambda j, g, s: (g, 0, 0))] + [spec] * 4,
            out_specs=[
                pl.BlockSpec((rows, step), lambda j, g, s: (0, j)),
                pl.BlockSpec((1, rows, step), lambda j, g, s: (g, 0, j)),
            ],
        ),
        out_shape=[
            jax.ShapeDtypeStruct((rows, cols), F32),
            jax.ShapeDtypeStruct((groups, rows, cols), BF16),
        ],
        compiler_params=params(),
        cost_estimate=cost(16 * groups * rows * cap * cols, 14 * groups * cap * cols + 4 * groups * rows * cols),
        name="merge_rows",
    )(place, inv, *keep, *got)


def finish_kernel(chunks, place_ref, *refs):
    own, got = refs[:chunks], refs[chunks : 2 * chunks]
    other_ref, occ_ref, virt_ref, out_ref = refs[2 * chunks :]
    groups = got[0].shape[0]
    cols = own[0].shape[1]
    for j in range(chunks):
        total = own[j][...]
        for k in range(1, groups):
            total = total + decode(got[j][lax.rem(place_ref[2] + k, groups)])
        span = slice(j * cols, (j + 1) * cols)
        denom = occ_ref[...] - virt_ref[:, span]
        out_ref[:, span] = (0.5 * total + other_ref[:, span]) / denom


def finish(place, own, got, other, occ_sum, virt_sum):
    rows, width = other.shape
    chunks = len(own)
    groups, _, cols = got[0].shape
    step = 64
    return pl.pallas_call(
        functools.partial(finish_kernel, chunks),
        grid_spec=pltpu.PrefetchScalarGridSpec(
            num_scalar_prefetch=1,
            grid=(rows // step,),
            in_specs=[pl.BlockSpec((step, cols), lambda i, s: (i, 0))] * chunks
            + [pl.BlockSpec((groups, step, cols), lambda i, s: (0, i, 0))] * chunks
            + [
                pl.BlockSpec((step, width), lambda i, s: (i, 0)),
                pl.BlockSpec((step, 1), lambda i, s: (i, 0)),
                pl.BlockSpec((1, width), lambda i, s: (0, 0)),
            ],
            out_specs=pl.BlockSpec((step, width), lambda i, s: (i, 0)),
        ),
        out_shape=jax.ShapeDtypeStruct((rows, width), F32),
        compiler_params=params(),
        cost_estimate=cost(40 * rows * width, (12 + 2 * groups) * rows * width),
        name="finish_rows",
    )(place, *own, *got, other, occ_sum, virt_sum)


def ranks(named, experts):
    blocks, top, rows = named.shape
    flat = named.reshape(blocks, top * rows)
    onehot = flat[:, :, None] == jnp.arange(experts, dtype=jnp.int32)
    before = jnp.tri(top * rows, k=-1, dtype=BF16)
    count = jnp.einsum("ij,bje->bie", before, onehot.astype(BF16), preferred_element_type=F32)
    shape = (blocks, top, rows, experts)
    return onehot.reshape(shape), count.astype(jnp.int32).reshape(shape)


def per_device(
    amplitudes, screen, integrals, other, occ_first, occ_second, virt_first, virt_second
):
    rows, top, width = amplitudes.shape
    n_pair = lax.axis_size("pair")
    n_virt = lax.axis_size("virt")
    cd_dev, _, cols = integrals.shape
    experts = cd_dev * n_pair
    cap = rows * top * 2 // experts
    quarter = width // n_virt
    pair = lax.axis_index("pair")
    virt = lax.axis_index("virt")
    low, high = pair % 2, pair // 2
    groups = n_pair // 2
    place = jnp.stack([virt, low, high]).astype(jnp.int32)

    named = screen.T[None]
    onehot, rank = ranks(named, experts)
    slot = jnp.sum(jnp.where(onehot, rank, 0), axis=3)[0]
    expert = named[0]
    where = expert // cd_dev * cap + slot
    tiles = lax.dynamic_slice_in_dim(amplitudes, virt * quarter, quarter, 2)
    tiles = tiles.transpose(1, 0, 2)

    every = lax.all_gather(screen, "pair")

    swap_low = [(i, i ^ 1) for i in range(n_pair)]

    lhs = []
    earlier = None
    for c in range(cd_dev):
        codes = jnp.where(expert % cd_dev == c, where, -1)
        buffer = pack(codes, tiles, n_pair * cap)
        if earlier is not None:
            buffer, earlier = lax.optimization_barrier((buffer, earlier))
            lhs[-1] = earlier
        earlier = lax.all_to_all(buffer, "pair", 0, 0, tiled=True)
        lhs.append(earlier)
    quarters = []
    for c in range(cd_dev):
        held = {0: lhs[c]}
        bit = n_virt // 2
        while bit:
            swap = [(i, i ^ bit) for i in range(n_virt)]
            held.update({at | bit: lax.ppermute(x, "virt", swap) for at, x in held.items()})
            bit //= 2
        quarters.append([held[at] for at in range(n_virt)])

    owners = lax.dynamic_index_in_dim(
        every.reshape(groups, 2, rows, top), low, 1, False
    )
    all_hot, all_rank = ranks(owners.transpose(0, 2, 1), experts)
    inv = jnp.sum(jnp.where(all_hot, all_rank + 1, 0), axis=1) - 1
    mine = lax.dynamic_slice_in_dim(inv, pair * cd_dev, cd_dev, 2)
    theirs = lax.dynamic_slice_in_dim(inv, (pair + 1 - 2 * low) * cd_dev, cd_dev, 2)
    inv = jnp.concatenate([mine, theirs], axis=2)

    keep, got = [], []
    part = cols // COL_CHUNKS
    for c in range(cd_dev):
        keep.append([])
        got.append([])
        for j in range(COL_CHUNKS):
            kept, sent = product(place, quarters[c], integrals, c, j * part, part, cap)
            keep[c].append(kept)
            got[c].append(lax.ppermute(sent, "pair", swap_low))

    own, back = [], []
    lines = [[i for i in range(n_pair) if i % 2 == side] for side in range(2)]
    for j in range(COL_CHUNKS):
        dense, sent = merge(
            place, inv, [keep[c][j] for c in range(cd_dev)], [got[c][j] for c in range(cd_dev)]
        )
        own.append(dense)
        back.append(lax.all_to_all(sent, "pair", 0, 0, tiled=True, axis_index_groups=lines))

    tile = virt_first.shape[1]
    tile_sq = tile * tile
    start_col = virt * cols
    tile_pair = start_col // tile_sq
    first_a = start_col % tile_sq // tile
    energy_a = lax.dynamic_slice(virt_first, (tile_pair, first_a), (1, cols // tile)).reshape(-1)
    energy_b = lax.dynamic_slice_in_dim(virt_second, tile_pair, 1, 0).reshape(-1)
    virt_sum = (energy_a[:, None] + energy_b[None, :]).reshape(1, cols)
    per_i = occ_second.shape[0]
    energy_i = lax.dynamic_slice_in_dim(occ_first, pair * (rows // per_i), rows // per_i, 0)
    occ_sum = (energy_i[:, None] + occ_second[None, :]).reshape(rows, 1)
    return finish(place, own, back, other, occ_sum, virt_sum)


def solution(mesh):
    return jax.shard_map(
        per_device,
        mesh=mesh,
        in_specs=(
            P("pair", None, None),
            P("pair", None),
            P("pair", None, "virt"),
            P("pair", "virt"),
            P(),
            P(),
            P(),
            P(),
        ),
        out_specs=P("pair", "virt"),
        check_vma=False,
    )
```

```python
import functools

import jax
import jax.numpy as jnp
from jax import lax
from jax.experimental import pallas as pl
from jax.experimental.pallas import tpu as pltpu
from jax.sharding import PartitionSpec as P

VMEM_LIMIT = 40 * 1024 * 1024
F32 = jnp.float32
BF16 = jnp.bfloat16
PARTS = (1, 2)
CHUNKS = (2, 3, 3)


def params():
    return pltpu.CompilerParams(vmem_limit_bytes=VMEM_LIMIT)


def cost(flops, nbytes):
    return pl.CostEstimate(flops=int(flops), bytes_accessed=int(nbytes), transcendentals=0)


def encode(v):
    w = v * 8.0
    sq = w * w
    quad = sq * sq
    return ((w * jnp.abs(w)) * (quad * sq)).astype(BF16)


def decode(code):
    c = code.astype(F32)
    a = jnp.abs(c)
    t = lax.rsqrt(jnp.maximum(a, 1e-37))
    u = lax.rsqrt(t)
    root = u * lax.rsqrt(u) * 0.125
    root = jnp.where(a < 1e-37, 0.0, root)
    return jnp.where(c < 0.0, -root, root)


def after(x, *earlier):
    earlier = [y for y in earlier if y is not None]
    return lax.optimization_barrier((x, *earlier))[0] if earlier else x


def pack_kernel(parts, codes_ref, tiles_ref, *outs):
    block = outs[0].shape[0]
    top, rows, _ = tiles_ref.shape
    want = lax.broadcasted_iota(jnp.int32, (block, rows), 0) + pl.program_id(0) * block
    for c in range(codes_ref.shape[0]):
        total = None
        for k in range(top):
            pick = (want == codes_ref[c, k : k + 1, :]).astype(F32).astype(BF16)
            part = jnp.dot(pick, tiles_ref[k], preferred_element_type=F32)
            total = part if total is None else total + part
        for out, (of, first, size) in zip(outs, parts):
            if of == c:
                out[...] = total[:, first : first + size].astype(BF16)


def pack(codes, tiles, n_slots, parts):
    top, rows, width = tiles.shape
    steps = 4
    return pl.pallas_call(
        functools.partial(pack_kernel, parts),
        grid=(steps,),
        in_specs=[
            pl.BlockSpec(codes.shape, lambda i: (0, 0, 0)),
            pl.BlockSpec((top, rows, width), lambda i: (0, 0, 0)),
        ],
        out_specs=[pl.BlockSpec((n_slots // steps, size), lambda i: (i, 0)) for _, _, size in parts],
        out_shape=[jax.ShapeDtypeStruct((n_slots, size), BF16) for _, _, size in parts],
        compiler_params=params(),
        cost_estimate=cost(4 * n_slots * top * rows * width, 8 * n_slots * width),
        name="pack_tiles",
    )(codes, tiles)


def product_kernel(offsets, place_ref, *refs):
    *parts, w_ref, keep_ref, send_ref, lhs_ref = refs
    half, cap, step = keep_ref.shape

    @pl.when(pl.program_id(0) == 0)
    def _():
        for part, (rel, stride, offset) in zip(parts, offsets):
            start = lax.bitwise_xor(place_ref[0], rel) * stride + offset
            size = part.shape[1]
            lhs_ref[:, pl.ds(pl.multiple_of(start, size), size)] = part[...]

    total = jnp.dot(lhs_ref[...], w_ref[0], preferred_element_type=F32)
    total = total.reshape(2 * half, cap, step)
    for g in range(half):
        first, second = total[2 * g], total[2 * g + 1]
        keep_ref[g] = jnp.where(place_ref[1] == 0, first, second)
        send_ref[g] = encode(jnp.where(place_ref[1] == 0, second, first))


def product(place, pieces, integrals, c, first, cols, cap, step):
    lhs = [piece for piece, _ in pieces]
    offsets = tuple(offset for _, offset in pieces)
    slots = lhs[0].shape[0]
    width = integrals.shape[1]
    half = slots // cap // 2
    base = first // step
    return pl.pallas_call(
        functools.partial(product_kernel, offsets),
        grid_spec=pltpu.PrefetchScalarGridSpec(
            num_scalar_prefetch=1,
            grid=(cols // step,),
            in_specs=[pl.BlockSpec(x.shape, lambda j, s: (0, 0)) for x in lhs]
            + [pl.BlockSpec((1, width, step), lambda j, s: (c, 0, base + j))],
            out_specs=[pl.BlockSpec((half, cap, step), lambda j, s: (0, 0, j))] * 2,
            scratch_shapes=[pltpu.VMEM((slots, width), BF16)],
        ),
        out_shape=[
            jax.ShapeDtypeStruct((half, cap, cols), F32),
            jax.ShapeDtypeStruct((half, cap, cols), BF16),
        ],
        compiler_params=params(),
        cost_estimate=cost(2 * slots * width * cols, 2 * width * cols + 2 * slots * width + 4 * slots * cols),
        name="tile_products",
    )(place, *lhs, integrals)


def dense_rows(inv_ref, values):
    rows = inv_ref.shape[1]
    slots = values.shape[0]
    cap = slots // 4
    lane = lax.broadcasted_iota(jnp.int32, (rows, slots), 1)
    hit = None
    for c in range(4):
        slot = inv_ref[0, :, c : c + 1]
        one = lane == jnp.where(slot < 0, -1, slot + c * cap)
        hit = one if hit is None else hit | one
    pick = hit.astype(F32).astype(BF16)
    high = values.astype(BF16)
    low = (values - high.astype(F32)).astype(BF16)
    dense = jnp.dot(pick, high, preferred_element_type=F32)
    return dense + jnp.dot(pick, low, preferred_element_type=F32)


def merge_kernel(place_ref, inv_ref, keep0, keep1, got0, got1, kept_ref, send_ref):
    values = [keep0[0], keep1[0], decode(got0[0]), decode(got1[0])]
    dense = dense_rows(inv_ref, jnp.concatenate(values, axis=0))

    @pl.when(pl.program_id(1) % 2 == 0)
    def _():
        kept_ref[0] = dense

    @pl.when(pl.program_id(1) % 2 == 1)
    def _():
        send_ref[0] = encode(dense)


def merge(place, inv, keep, got):
    groups, cap, cols = keep[0].shape
    rows = inv.shape[1]
    step = cols
    spec = pl.BlockSpec((1, cap, step), lambda j, r, s: (s[2] ^ r, 0, j))
    half = pl.BlockSpec((1, rows, step), lambda j, r, s: (r // 2, 0, j))
    shape = (groups // 2, rows, cols)
    return pl.pallas_call(
        merge_kernel,
        grid_spec=pltpu.PrefetchScalarGridSpec(
            num_scalar_prefetch=1,
            grid=(cols // step, groups),
            in_specs=[pl.BlockSpec((1, rows, 4), lambda j, r, s: (s[2] ^ r, 0, 0))] + [spec] * 4,
            out_specs=[half, half],
        ),
        out_shape=[jax.ShapeDtypeStruct(shape, F32), jax.ShapeDtypeStruct(shape, BF16)],
        compiler_params=params(),
        cost_estimate=cost(16 * groups * rows * cap * cols, 14 * groups * cap * cols + 4 * groups * rows * cols),
        name="merge_rows",
    )(place, inv, *keep, *got)


def halve_kernel(place_ref, kept_ref, got_ref, out_ref, send_ref):
    out_ref[0] = kept_ref[0] + decode(got_ref[0])
    send_ref[0] = encode(kept_ref[1] + decode(got_ref[1]))


def halve(place, kept, got):
    count, rows, cols = kept.shape
    step = rows // 2
    two = pl.BlockSpec((2, step, cols), lambda i, r, s: (i, r, 0))
    one = pl.BlockSpec((1, step, cols), lambda i, r, s: (i, r, 0))
    shape = (count // 2, rows, cols)
    return pl.pallas_call(
        halve_kernel,
        grid_spec=pltpu.PrefetchScalarGridSpec(
            num_scalar_prefetch=1,
            grid=(count // 2, rows // step),
            in_specs=[two, two],
            out_specs=[one, one],
        ),
        out_shape=[jax.ShapeDtypeStruct(shape, F32), jax.ShapeDtypeStruct(shape, BF16)],
        compiler_params=params(),
        cost_estimate=cost(30 * count * rows * cols, 9 * count * rows * cols),
        name="halve_rows",
    )(place, kept, got)


def finish_kernel(place_ref, own_ref, got_ref, other_ref, occ_ref, virt_ref, *refs):
    total = own_ref[0] + decode(got_ref[0])
    denom = occ_ref[...] - virt_ref[...]
    refs[-1][...] = (0.5 * total + other_ref[...]) / denom


def finish(place, own, got, other, occ_sum, virt_sum, first, step, out):
    rows, width = other.shape
    cols = own.shape[2]
    base = first // step
    here = pl.BlockSpec((1, rows, step), lambda j, s: (0, 0, j))
    there = pl.BlockSpec((rows, step), lambda j, s: (0, base + j))
    earlier = [] if out is None else [out]
    return pl.pallas_call(
        finish_kernel,
        grid_spec=pltpu.PrefetchScalarGridSpec(
            num_scalar_prefetch=1,
            grid=(cols // step,),
            in_specs=[
                here,
                here,
                there,
                pl.BlockSpec((rows, 1), lambda j, s: (0, 0)),
                pl.BlockSpec((1, step), lambda j, s: (0, base + j)),
            ]
            + [pl.BlockSpec(memory_space=pl.ANY)] * len(earlier),
            out_specs=there,
        ),
        out_shape=jax.ShapeDtypeStruct((rows, width), F32),
        input_output_aliases={6: 0} if earlier else {},
        compiler_params=params(),
        cost_estimate=cost(40 * rows * cols, 14 * rows * cols),
        name="finish_rows",
    )(place, own, got, other, occ_sum, virt_sum, *earlier)


def ranks(named, experts):
    blocks, top, rows = named.shape
    flat = named.reshape(blocks, top * rows)
    onehot = flat[:, :, None] == jnp.arange(experts, dtype=jnp.int32)
    before = jnp.tri(top * rows, k=-1, dtype=BF16)
    count = jnp.einsum("ij,bje->bie", before, onehot.astype(BF16), preferred_element_type=F32)
    shape = (blocks, top, rows, experts)
    return onehot.reshape(shape), count.astype(jnp.int32).reshape(shape)


def per_device(
    amplitudes, screen, integrals, other, occ_first, occ_second, virt_first, virt_second
):
    rows, top, width = amplitudes.shape
    n_pair = lax.axis_size("pair")
    n_virt = lax.axis_size("virt")
    cd_dev, _, cols = integrals.shape
    experts = cd_dev * n_pair
    cap = rows * top * 2 // experts
    quarter = width // n_virt
    pair = lax.axis_index("pair")
    virt = lax.axis_index("virt")
    low, high = pair % 2, pair // 2
    groups = n_pair // 2
    place = jnp.stack([virt, low, high]).astype(jnp.int32)

    named = screen.T[None]
    onehot, rank = ranks(named, experts)
    slot = jnp.sum(jnp.where(onehot, rank, 0), axis=3)[0]
    expert = named[0]
    where = expert // cd_dev * cap + slot
    tiles = lax.dynamic_slice_in_dim(amplitudes, virt * quarter, quarter, 2)
    tiles = tiles.transpose(1, 0, 2)

    every = [screen.T]
    for k in range(1, groups):
        around = [(i, (i + 2 * k) % n_pair) for i in range(n_pair)]
        every.append(lax.ppermute(every[0], "pair", around))

    swap_low = [(i, i ^ 1) for i in range(n_pair)]

    parts = []
    for c in range(cd_dev):
        size = quarter // PARTS[c]
        parts += [(c, first, size) for first in range(0, quarter, size)]
    codes = jnp.stack([jnp.where(expert % cd_dev == c, where, -1) for c in range(cd_dev)])
    arrived = []
    for x in pack(codes, tiles, n_pair * cap, parts):
        arrived.append(lax.all_to_all(after(x, *arrived[-1:]), "pair", 0, 0, tiled=True))

    owners = jnp.roll(jnp.stack(every[::-1]), high + 1, axis=0)
    all_hot, all_rank = ranks(owners, experts)
    inv = jnp.sum(jnp.where(all_hot, all_rank + 1, 0), axis=1) - 1
    mine = lax.dynamic_slice_in_dim(inv, pair * cd_dev, cd_dev, 2)
    theirs = lax.dynamic_slice_in_dim(inv, (pair + 1 - 2 * low) * cd_dev, cd_dev, 2)
    inv = jnp.concatenate([mine, theirs], axis=2)

    def share(x, *waits):
        held = {0: x}
        bit = n_virt // 2
        while bit:
            swap = [(i, i ^ bit) for i in range(n_virt)]
            if bit == 1:
                held = {at: after(x, *waits) if at else x for at, x in held.items()}
            held.update({at | bit: lax.ppermute(x, "virt", swap) for at, x in held.items()})
            bit //= 2
        return held

    def share(x, *waits):
        held = {0: x}
        bit = n_virt // 2
        while bit:
            swap = [(i, i ^ bit) for i in range(n_virt)]
            if bit == 1:
                held = {at: after(x, *waits) if at else x for at, x in held.items()}
            held.update({at | bit: lax.ppermute(x, "virt", swap) for at, x in held.items()})
            bit //= 2
        return held

    def hop(x, bit):
        return lax.ppermute(x, "pair", [(i, i ^ bit) for i in range(n_pair)])

    unit = cols // sum(CHUNKS)
    spans = [(unit * sum(CHUNKS[:j]), unit * size) for j, size in enumerate(CHUNKS)]
    keep, got = [[] for _ in spans], [[] for _ in spans]
    count = len(spans)
    made, moved = [], []

    def make(c, j, pieces, *waits):
        first, size = spans[j]
        waits = [*made[-1:], *moved[-2:-1], *waits]
        kept, sent = product(after(place, *waits), pieces, integrals, c, first, size, cap, unit)
        made.append(kept)
        moved.append(hop(sent, 1))
        keep[j].append(kept)
        got[j].append(moved[-1])

    pieces = [[], []]
    for n, ((c, first, _), x) in enumerate(zip(parts, arrived)):
        held = share(x, *(made[-1:] if n + 1 == len(parts) else []))
        pieces[c] += [(y, (at, quarter, first)) for at, y in held.items()]
        if n == 0:
            for j in range(count):
                make(0, j, pieces[0], arrived[1 if j + 1 < count else -1])
    computed = made[-1]

    levels = groups.bit_length() - 1
    state = {}

    def advance(j, level, *waits):
        if level == 0:
            kept, sent = merge(after(place, *waits), inv, keep[j], got[j])
        else:
            kept, sent = halve(after(place, *waits), *state[j])
        state[j] = (kept, hop(sent, 2 << level))
        return kept

    make(1, 0, pieces[1], computed)
    computed = made[-1]
    for turn in range(count + levels):
        if turn + 1 < count:
            make(1, turn + 1, pieces[1], computed)
            computed = made[-1]
        for level in range(levels):
            j = turn - level
            if 0 <= j < count:
                computed = advance(j, level, computed)

    tile = virt_first.shape[1]
    tile_sq = tile * tile
    start_col = virt * cols
    tile_pair = start_col // tile_sq
    first_a = start_col % tile_sq // tile
    energy_a = lax.dynamic_slice(virt_first, (tile_pair, first_a), (1, cols // tile)).reshape(-1)
    energy_b = lax.dynamic_slice_in_dim(virt_second, tile_pair, 1, 0).reshape(-1)
    virt_sum = (energy_a[:, None] + energy_b[None, :]).reshape(1, cols)
    per_i = occ_second.shape[0]
    energy_i = lax.dynamic_slice_in_dim(occ_first, pair * (rows // per_i), rows // per_i, 0)
    occ_sum = (energy_i[:, None] + occ_second[None, :]).reshape(rows, 1)
    out = None
    for j, (first, _) in enumerate(spans):
        out = finish(place, *state[j], other, occ_sum, virt_sum, first, unit, out)
    return out


def solution(mesh):
    return jax.shard_map(
        per_device,
        mesh=mesh,
        in_specs=(
            P("pair", None, None),
            P("pair", None),
            P("pair", None, "virt"),
            P("pair", "virt"),
            P(),
            P(),
            P(),
            P(),
        ),
        out_specs=P("pair", "virt"),
        check_vma=False,
    )
```

```python
import functools
import math

import jax
import jax.numpy as jnp
from jax import lax
from jax.experimental import pallas as pl
from jax.experimental.pallas import tpu as pltpu
from jax.sharding import PartitionSpec as P

MIB = 1024 * 1024
F32 = jnp.float32
BF16 = jnp.bfloat16
CHUNKS = (4, 4)
HEAVY = 1e11
EARLY_JOINED = True


def params(mib=16):
    return pltpu.CompilerParams(vmem_limit_bytes=mib * MIB)


def cost(flops, nbytes):
    return pl.CostEstimate(flops=int(flops), bytes_accessed=int(nbytes), transcendentals=0)


def encode(v):
    w = v * 8.0
    sq = w * w
    quad = sq * sq
    return ((w * jnp.abs(w)) * (quad * sq)).astype(BF16)


def decode(code):
    c = code.astype(F32)
    a = jnp.abs(c)
    t = lax.rsqrt(jnp.maximum(a, 1e-37))
    u = lax.rsqrt(t)
    root = u * lax.rsqrt(u) * 0.125
    root = jnp.where(a < 1e-37, 0.0, root)
    return jnp.where(c < 0.0, -root, root)


def after(x, *earlier):
    earlier = [y for y in earlier if y is not None]
    return lax.optimization_barrier((x, *earlier))[0] if earlier else x


def pin_kernel(place_ref, out_ref):
    out_ref[0] = place_ref[0]


def pin(place, *earlier):
    scalar = pl.BlockSpec(memory_space=pltpu.SMEM)
    return pl.pallas_call(
        pin_kernel,
        in_specs=[scalar],
        out_specs=scalar,
        out_shape=jax.ShapeDtypeStruct((1,), jnp.int32),
        cost_estimate=cost(HEAVY, 8),
        name="pin",
    )(after(place, *earlier))


def pack_kernel(codes_ref, tiles_ref, *outs):
    top, rows, _ = tiles_ref.shape
    block = outs[0].shape[0]
    lane = lax.broadcasted_iota(jnp.int32, (block, rows), 0)
    for at, out in enumerate(outs):
        total = None
        for k in range(top):
            pick = (lane == codes_ref[k : k + 1, :] - at * block).astype(F32).astype(BF16)
            part = jnp.dot(pick, tiles_ref[k], preferred_element_type=F32)
            total = part if total is None else total + part
        out[...] = total.astype(BF16)


def pack(codes, tiles, count, block):
    top, rows, width = tiles.shape
    n_slots = count * block
    return pl.pallas_call(
        pack_kernel,
        out_shape=[jax.ShapeDtypeStruct((block, width), BF16)] * count,
        compiler_params=params(),
        cost_estimate=cost(0, 0),
        name="pack_tiles",
    )(codes, tiles)


def product_kernel(layout, place_ref, *refs):
    *parts, w_ref, keep_ref, send_ref = refs
    cap = keep_ref.shape[2]
    sides = {}
    for part, (rel, ks) in zip(parts, layout):
        sides.setdefault(rel, []).append((part, ks))
    total = None
    for rel, blocks in sides.items():
        lhs = [part[:, 0].reshape(-1, part.shape[3]) for part, _ in blocks]
        lhs = jnp.concatenate(lhs, axis=0) if len(lhs) > 1 else lhs[0]
        size = lhs.shape[1]
        start = pl.multiple_of(lax.bitwise_xor(place_ref[0], rel) * size, size)
        more = jnp.dot(lhs, w_ref[0, pl.ds(start, size), :], preferred_element_type=F32)
        total = more if total is None else total + more
    for n, k in enumerate([k for _, ks in sides[0] for k in ks]):
        block = total[n * cap : (n + 1) * cap]
        if k % 2:
            send_ref[0, k // 4] = encode(block)
        else:
            keep_ref[0, k // 4] = block


def product(place, pieces, integrals, first, cols, cap):
    lhs = [piece[0] for piece in pieces]
    layout = tuple(piece[1:] for piece in pieces)
    experts, width, _ = integrals.shape
    half = sum(x.shape[0] for x, rel, _ in pieces if rel == 0) // 2
    step = math.gcd(first, cols) if first else cols
    base, steps = first // step, cols // step
    out = pl.BlockSpec((1, half, cap, step), lambda t, s: (t // steps, 0, 0, t % steps))
    shape = (experts, half, cap, cols)
    return pl.pallas_call(
        functools.partial(product_kernel, layout),
        grid_spec=pltpu.PrefetchScalarGridSpec(
            num_scalar_prefetch=1,
            grid=(experts * steps,),
            in_specs=[
                pl.BlockSpec((x.shape[0], 1, *x.shape[2:]), lambda t, s: (0, t // steps, 0, 0))
                for x in lhs
            ]
            + [pl.BlockSpec((1, width, step), lambda t, s: (t // steps, 0, base + t % steps))],
            out_specs=[out, out],
        ),
        out_shape=[jax.ShapeDtypeStruct(shape, F32), jax.ShapeDtypeStruct(shape, BF16)],
        compiler_params=params(36),
        cost_estimate=cost(HEAVY, 2 * experts * width * cols),
        name="tile_products",
    )(place, *lhs, integrals)


def dense_rows(inv_ref, values):
    rows = inv_ref.shape[1]
    slots = values.shape[0]
    cap = slots // 4
    lane = lax.broadcasted_iota(jnp.int32, (rows, slots), 1)
    hit = None
    for c in range(4):
        slot = inv_ref[0, :, c : c + 1]
        one = lane == jnp.where(slot < 0, -1, slot + c * cap)
        hit = one if hit is None else hit | one
    pick = hit.astype(F32).astype(BF16)
    high = values.astype(BF16)
    low = (values - high.astype(F32)).astype(BF16)
    dense = jnp.dot(pick, high, preferred_element_type=F32)
    return dense + jnp.dot(pick, low, preferred_element_type=F32)


def merge_kernel(place_ref, inv_ref, keep0, keep1, got0, got1, *refs):
    values = [keep0[0, 0], keep1[0, 0], decode(got0[0, 0]), decode(got1[0, 0])]
    dense = dense_rows(inv_ref, jnp.concatenate(values, axis=0))
    if len(refs) == 1:
        refs[0][0] = encode(dense)
        return
    near_ref, kept_ref, send_ref = refs
    dense = dense + decode(near_ref[0])

    @pl.when(pl.program_id(0) % 2 == 0)
    def _():
        kept_ref[0] = dense

    @pl.when(pl.program_id(0) % 2 == 1)
    def _():
        send_ref[0] = encode(dense)


def merge(place, inv, keep, got, near):
    _, half, cap, cols = keep.shape
    rows = inv.shape[1]
    odd = near is None

    def spec(c):
        return pl.BlockSpec((1, 1, cap, cols), lambda i, s: (c, i, 0, 0))

    each = pl.BlockSpec((1, rows, cols), lambda i, s: (i, 0, 0))
    second = pl.BlockSpec((1, rows, cols), lambda i, s: (i // 2, 0, 0))
    shape = functools.partial(jax.ShapeDtypeStruct, (half // 2, rows, cols))
    return pl.pallas_call(
        merge_kernel,
        grid_spec=pltpu.PrefetchScalarGridSpec(
            num_scalar_prefetch=1,
            grid=(half,),
            in_specs=[pl.BlockSpec((1, rows, 4), lambda i, s: (2 * i + odd, 0, 0))]
            + [spec(0), spec(1)] * 2
            + [each] * (not odd),
            out_specs=each if odd else [second, second],
        ),
        out_shape=jax.ShapeDtypeStruct((half, rows, cols), BF16) if odd else [shape(F32), shape(BF16)],
        compiler_params=params(),
        cost_estimate=cost(0, 0),
        name="merge_rows",
    )(place, inv, keep, keep, got, got, *([] if odd else [near]))


def halve_kernel(kept_ref, got_ref, out_ref, send_ref):
    out_ref[0] = kept_ref[0] + decode(got_ref[0])
    send_ref[0] = encode(kept_ref[1] + decode(got_ref[1]))


def halve(kept, got):
    count, rows, cols = kept.shape
    step = rows // 2
    two = pl.BlockSpec((2, step, cols), lambda i, r: (i, r, 0))
    one = pl.BlockSpec((1, step, cols), lambda i, r: (i, r, 0))
    shape = (count // 2, rows, cols)
    return pl.pallas_call(
        halve_kernel,
        grid=(count // 2, rows // step),
        in_specs=[two, two],
        out_specs=[one, one],
        out_shape=[jax.ShapeDtypeStruct(shape, F32), jax.ShapeDtypeStruct(shape, BF16)],
        compiler_params=params(),
        cost_estimate=cost(0, 0),
        name="halve_rows",
    )(kept, got)


def finish_kernel(own_ref, got_ref, other_ref, occ_ref, virt_ref, *refs):
    total = own_ref[0] + decode(got_ref[0])
    denom = occ_ref[...] - virt_ref[...]
    refs[-1][...] = (0.5 * total + other_ref[...]) / denom


def finish(own, got, other, occ_sum, virt_sum, first, step, out):
    rows, width = other.shape
    cols = own.shape[2]
    base = first // step
    here = pl.BlockSpec((1, rows, step), lambda j: (0, 0, j))
    there = pl.BlockSpec((rows, step), lambda j: (0, base + j))
    earlier = [] if out is None else [out]
    return pl.pallas_call(
        finish_kernel,
        grid=(cols // step,),
        in_specs=[
            here,
            here,
            there,
            pl.BlockSpec((rows, 1), lambda j: (0, 0)),
            pl.BlockSpec((1, step), lambda j: (0, base + j)),
        ]
        + [pl.BlockSpec(memory_space=pl.ANY)] * len(earlier),
        out_specs=there,
        out_shape=jax.ShapeDtypeStruct((rows, width), F32),
        input_output_aliases={5: 0} if earlier else {},
        compiler_params=params(),
        cost_estimate=cost(0, 0),
        name="finish_rows",
    )(own, got, other, occ_sum, virt_sum, *earlier)


def ranks(named, experts):
    blocks, top, rows = named.shape
    flat = named.reshape(blocks, top * rows)
    onehot = flat[:, :, None] == jnp.arange(experts, dtype=jnp.int32)
    before = jnp.tri(top * rows, k=-1, dtype=BF16)
    count = jnp.einsum("ij,bje->bie", before, onehot.astype(BF16), preferred_element_type=F32)
    shape = (blocks, top, rows, experts)
    return onehot.reshape(shape), count.astype(jnp.int32).reshape(shape)


def per_device(
    amplitudes, screen, integrals, other, occ_first, occ_second, virt_first, virt_second
):
    rows, top, width = amplitudes.shape
    n_pair = lax.axis_size("pair")
    n_virt = lax.axis_size("virt")
    cd_dev, _, cols = integrals.shape
    experts = cd_dev * n_pair
    cap = rows * top * 2 // experts
    quarter = width // n_virt
    pair = lax.axis_index("pair")
    virt = lax.axis_index("virt")
    groups = n_pair // 2
    place = virt.astype(jnp.int32).reshape(1)
    block = cd_dev * cap

    def hop(x, bits):
        return lax.ppermute(x, "pair", [(i, i ^ bits) for i in range(n_pair)])

    def swap(x, bits):
        return lax.ppermute(x, "virt", [(i, i ^ bits) for i in range(n_virt)])

    named = screen.T
    onehot, rank = ranks(named[None], experts)
    slot = jnp.sum(jnp.where(onehot, rank, 0), axis=3)[0]
    partner = lax.bitwise_xor(named // cd_dev, pair.astype(jnp.int32))
    codes = partner * block + named % cd_dev * cap + slot
    tiles = lax.dynamic_slice_in_dim(amplitudes, virt * quarter, quarter, 2)
    tiles = tiles.transpose(1, 0, 2)
    packed = pack(codes, tiles, n_pair, block)

    early = [k for k in range(n_pair) if k // 2 % 2]
    late = [k for k in range(1, n_pair) if not k // 2 % 2]
    far = [k for ks in (early, late) for k in ks if k >= n_pair // 2]
    close = [k for ks in (early, late) for k in ks if k < n_pair // 2]
    held = {k: {0: x} for k, x in enumerate(packed)}
    shared = []

    def share(k, *waits):
        bits = n_virt // 2
        while bits > 1:
            more = {at | bits: swap(after(x, *waits), bits) for at, x in held[k].items()}
            held[k].update(more)
            bits //= 2
        shared.append(list(held[k].values())[-1])

    def send(ks, n):
        if n < len(ks):
            waits = [held[ks[n - 1]][0]] if n else []
            held[ks[n]] = {0: hop(after(packed[ks[n]], *waits), ks[n])}
            return [held[ks[n]][0]]
        return []

    share(0)
    for n in range(len(far) - 1):
        under_way = send(far, n) + send(close, n) + shared[-1:]
        if n:
            share(close[n - 1])
            share(far[n - 1])
            under_way += shared[-2:]
        if n == 1:
            at = after(named, held[close[0]][0])
            owners = [named] + [hop(at, 2 * r) for r in range(1, groups)]
            under_way += owners[1:]
        place = pin(place, *under_way)
    shares = [0] + [k for both in zip(far, close) for k in both] + far[-1:]

    all_hot, all_rank = ranks(jnp.stack(owners), experts)
    inv = jnp.sum(jnp.where(all_hot, all_rank + 1, 0), axis=1) - 1
    mine = lax.dynamic_slice_in_dim(inv, pair * cd_dev, cd_dev, 2)
    theirs = lax.dynamic_slice_in_dim(inv, lax.bitwise_xor(pair, 1) * cd_dev, cd_dev, 2)
    inv = jnp.concatenate([mine, theirs], axis=2)

    unit = cols // sum(CHUNKS)
    spans = [(unit * sum(CHUNKS[:j]), unit * size) for j, size in enumerate(CHUNKS)]
    count = len(spans)
    levels = groups.bit_length() - 1
    made, moved, near, state = {}, {}, {}, {}
    done, hops = [], []

    def make(pieces, j, *waits):
        at = after(place, *done[-1:], *hops[-2:-1], *waits)
        kept, sent = product(at, pieces, integrals, *spans[j], cap)
        made[j], moved[j] = kept, hop(sent, 1)
        hops.append(moved[j])
        done.append(kept)

    def first_rows(j):
        sent = merge(after(place, *done[-1:]), inv, made[j], moved[j], None)
        near[j] = hop(sent, 2)
        done.append(sent)

    def second_rows(j):
        kept, sent = merge(after(place, *done[-1:]), inv, made[j], moved[j], near[j])
        state[j] = (kept, hop(sent, 4))
        done.append(kept)

    def more_rows(j, level):
        kept, sent = halve(after(state[j][0], *done[-1:]), state[j][1])
        state[j] = (kept, hop(sent, 2 << level))
        done.append(kept)

    rows_early = [k for k in shares if k in early]
    rows_late = [k for k in shares if k not in early]

    def gather(ks, joined, *waits):
        pieces = []
        for ks in [ks] if joined else [[k] for k in ks]:
            for at in held[ks[0]]:
                x = jnp.concatenate([held[k][at] for k in ks])
                if at and ks[-1] == far[-1]:
                    x = after(x, *waits)
                for bit, y in ((0, x), (1, swap(x, 1))):
                    pieces.append((y.reshape(len(ks), cd_dev, cap, quarter), at | bit, tuple(ks)))
        return pieces

    last = len(far) - 1
    send(far, last)
    share(close[last - 1])
    share(far[last - 1])
    pieces = gather(rows_early, EARLY_JOINED)
    make(pieces, 0)
    waits = [held[far[last]][0], *shared[-2:]]
    for j in range(1, count):
        make(pieces, j, *waits)
        if j == 1:
            share(far[last])
        waits = shared[-1:]
        first_rows(j - 1)
    pieces = gather(rows_late, False, made[1])
    make(pieces, 0)
    first_rows(count - 1)
    for j in range(count):
        if j + 1 < count:
            make(pieces, j + 1, near[j])
        second_rows(j)
    for level in range(2, levels):
        for j in range(count):
            more_rows(j, level)

    tile = virt_first.shape[1]
    tile_sq = tile * tile
    start_col = virt * cols
    tile_pair = start_col // tile_sq
    first_a = start_col % tile_sq // tile
    energy_a = lax.dynamic_slice(virt_first, (tile_pair, first_a), (1, cols // tile)).reshape(-1)
    energy_b = lax.dynamic_slice_in_dim(virt_second, tile_pair, 1, 0).reshape(-1)
    virt_sum = (energy_a[:, None] + energy_b[None, :]).reshape(1, cols)
    per_i = occ_second.shape[0]
    energy_i = lax.dynamic_slice_in_dim(occ_first, pair * (rows // per_i), rows // per_i, 0)
    occ_sum = (energy_i[:, None] + occ_second[None, :]).reshape(rows, 1)
    out = None
    for j, (first, _) in enumerate(spans):
        own = after(state[j][0], *done[-1:])
        out = finish(own, state[j][1], other, occ_sum, virt_sum, first, unit, out)
    return out


def solution(mesh):
    return jax.shard_map(
        per_device,
        mesh=mesh,
        in_specs=(
            P("pair", None, None),
            P("pair", None),
            P("pair", None, "virt"),
            P("pair", "virt"),
            P(),
            P(),
            P(),
            P(),
        ),
        out_specs=P("pair", "virt"),
        check_vma=False,
    )
```

```python
import functools
import math

import jax
import jax.numpy as jnp
from jax import lax
from jax.experimental import pallas as pl
from jax.experimental.pallas import tpu as pltpu
from jax.sharding import PartitionSpec as P

MIB = 1024 * 1024
F32 = jnp.float32
BF16 = jnp.bfloat16
CHUNKS = (4, 4)
SPLIT = (2, 2)
GATES = {("M", 2): (0,)}
HM = 2
HEAVY = 1e11
EARLY_JOINED = True
MAX_STEP = 512
SECOND = 8e9


def params(mib=16):
    return pltpu.CompilerParams(vmem_limit_bytes=mib * MIB)


def cost(flops, nbytes):
    return pl.CostEstimate(flops=int(flops), bytes_accessed=int(nbytes), transcendentals=0)


def encode(v):
    w = v * 8.0
    sq = w * w
    quad = sq * sq
    return ((w * jnp.abs(w)) * (quad * sq)).astype(BF16)


def decode(code):
    c = code.astype(F32)
    a = jnp.abs(c)
    t = lax.rsqrt(jnp.maximum(a, 1e-37))
    u = lax.rsqrt(t)
    root = u * lax.rsqrt(u) * 0.125
    root = jnp.where(a < 1e-37, 0.0, root)
    return jnp.where(c < 0.0, -root, root)


def after(x, *earlier):
    earlier = [y for y in earlier if y is not None]
    return lax.optimization_barrier((x, *earlier))[0] if earlier else x


def pin_kernel(place_ref, out_ref):
    out_ref[0] = place_ref[0]


def pin(place, *earlier):
    scalar = pl.BlockSpec(memory_space=pltpu.SMEM)
    return pl.pallas_call(
        pin_kernel,
        in_specs=[scalar],
        out_specs=scalar,
        out_shape=jax.ShapeDtypeStruct((1,), jnp.int32),
        cost_estimate=cost(HEAVY, 8),
        name="pin",
    )(after(place, *earlier))


def pack_kernel(codes_ref, tiles_ref, *outs):
    top, rows, _ = tiles_ref.shape
    block = outs[0].shape[0]
    lane = lax.broadcasted_iota(jnp.int32, (block, rows), 0)
    for at, out in enumerate(outs):
        total = None
        for k in range(top):
            pick = (lane == codes_ref[k : k + 1, :] - at * block).astype(F32).astype(BF16)
            part = jnp.dot(pick, tiles_ref[k], preferred_element_type=F32)
            total = part if total is None else total + part
        out[...] = total.astype(BF16)


def pack(codes, tiles, count, block):
    top, rows, width = tiles.shape
    n_slots = count * block
    return pl.pallas_call(
        pack_kernel,
        out_shape=[jax.ShapeDtypeStruct((block, width), BF16)] * count,
        compiler_params=params(),
        cost_estimate=cost(0, 0),
        name="pack_tiles",
    )(codes, tiles)


def product_kernel(layout, place_ref, *refs):
    *parts, w_ref, keep_ref, send_ref = refs
    cap = keep_ref.shape[2]
    sides = {}
    for part, (rel, ks) in zip(parts, layout):
        sides.setdefault(rel, []).append((part, ks))
    total = None
    for rel, blocks in sides.items():
        lhs = [part[:, 0].reshape(-1, part.shape[3]) for part, _ in blocks]
        lhs = jnp.concatenate(lhs, axis=0) if len(lhs) > 1 else lhs[0]
        size = lhs.shape[1]
        start = pl.multiple_of(lax.bitwise_xor(place_ref[0], rel) * size, size)
        more = jnp.dot(lhs, w_ref[0, pl.ds(start, size), :], preferred_element_type=F32)
        total = more if total is None else total + more
    for n, k in enumerate([k for _, ks in sides[0] for k in ks]):
        block = total[n * cap : (n + 1) * cap]
        if k % 2:
            send_ref[0, k // 4] = encode(block)
        else:
            keep_ref[0, k // 4] = block


def product(place, pieces, integrals, first, cols, cap, flops):
    lhs = [piece[0] for piece in pieces]
    layout = tuple(piece[1:] for piece in pieces)
    experts, width, _ = integrals.shape
    half = sum(x.shape[0] for x, rel, _ in pieces if rel == 0) // 2
    step = math.gcd(first, cols, MAX_STEP)
    base, steps = first // step, cols // step
    out = pl.BlockSpec((1, half, cap, step), lambda t, s: (t // steps, 0, 0, t % steps))
    shape = (experts, half, cap, cols)
    return pl.pallas_call(
        functools.partial(product_kernel, layout),
        grid_spec=pltpu.PrefetchScalarGridSpec(
            num_scalar_prefetch=1,
            grid=(experts * steps,),
            in_specs=[
                pl.BlockSpec((x.shape[0], 1, *x.shape[2:]), lambda t, s: (0, t // steps, 0, 0))
                for x in lhs
            ]
            + [pl.BlockSpec((1, width, step), lambda t, s: (t // steps, 0, base + t % steps))],
            out_specs=[out, out],
        ),
        out_shape=[jax.ShapeDtypeStruct(shape, F32), jax.ShapeDtypeStruct(shape, BF16)],
        compiler_params=params(36),
        cost_estimate=cost(flops, 0),
        name="tile_products",
    )(place, *lhs, integrals)


def dense_rows(inv_ref, values):
    rows = inv_ref.shape[1]
    slots = values.shape[0]
    cap = slots // 4
    lane = lax.broadcasted_iota(jnp.int32, (rows, slots), 1)
    hit = None
    for c in range(4):
        slot = inv_ref[0, :, c : c + 1]
        one = lane == jnp.where(slot < 0, -1, slot + c * cap)
        hit = one if hit is None else hit | one
    pick = hit.astype(F32).astype(BF16)
    high = values.astype(BF16)
    low = (values - high.astype(F32)).astype(BF16)
    dense = jnp.dot(pick, high, preferred_element_type=F32)
    return dense + jnp.dot(pick, low, preferred_element_type=F32)


def merge_kernel(place_ref, inv_ref, keep0, keep1, got0, got1, *refs):
    values = [keep0[0, 0], keep1[0, 0], decode(got0[0, 0]), decode(got1[0, 0])]
    dense = dense_rows(inv_ref, jnp.concatenate(values, axis=0))
    if len(refs) == 1:
        refs[0][0] = encode(dense)
        return
    near_ref, kept_ref, send_ref = refs
    dense = dense + decode(near_ref[0])

    @pl.when(pl.program_id(0) % 2 == 0)
    def _():
        kept_ref[0] = dense

    @pl.when(pl.program_id(0) % 2 == 1)
    def _():
        send_ref[0] = encode(dense)


def merge(place, inv, keep, got, near, at=0, flops=0):
    _, half, cap, cols = keep.shape
    rows = inv.shape[1]
    odd = near is None

    def spec(c):
        return pl.BlockSpec((1, 1, cap, cols), lambda i, s: (c, i, 0, 0))

    each = pl.BlockSpec((1, rows, cols), lambda i, s: (i, 0, 0))
    second = pl.BlockSpec((1, rows, cols), lambda i, s: (i // 2, 0, 0))
    shape = functools.partial(jax.ShapeDtypeStruct, (half // 2, rows, cols))
    return pl.pallas_call(
        merge_kernel,
        grid_spec=pltpu.PrefetchScalarGridSpec(
            num_scalar_prefetch=1,
            grid=(half,),
            in_specs=[pl.BlockSpec((1, rows, 4), lambda i, s: (2 * i + odd, 0, 0))]
            + [spec(0), spec(1)] * 2
            + [pl.BlockSpec((1, rows, cols), lambda i, s: (i, 0, at))] * (not odd),
            out_specs=each if odd else [second, second],
        ),
        out_shape=jax.ShapeDtypeStruct((half, rows, cols), BF16) if odd else [shape(F32), shape(BF16)],
        compiler_params=params(),
        cost_estimate=cost(flops, 0),
        name="merge_rows",
    )(place, inv, keep, keep, got, got, *([] if odd else [near]))


def halve_kernel(kept_ref, got_ref, out_ref, send_ref):
    out_ref[0] = kept_ref[0] + decode(got_ref[0])
    send_ref[0] = encode(kept_ref[1] + decode(got_ref[1]))


def halve(kept, got):
    count, rows, cols = kept.shape
    step = rows // 2
    two = pl.BlockSpec((2, step, cols), lambda i, r: (i, r, 0))
    one = pl.BlockSpec((1, step, cols), lambda i, r: (i, r, 0))
    shape = (count // 2, rows, cols)
    return pl.pallas_call(
        halve_kernel,
        grid=(count // 2, rows // step),
        in_specs=[two, two],
        out_specs=[one, one],
        out_shape=[jax.ShapeDtypeStruct(shape, F32), jax.ShapeDtypeStruct(shape, BF16)],
        compiler_params=params(),
        cost_estimate=cost(0, 0),
        name="halve_rows",
    )(kept, got)


def finish_kernel(own_ref, got_ref, other_ref, occ_ref, virt_ref, *refs):
    total = own_ref[0] + decode(got_ref[0])
    denom = occ_ref[...] - virt_ref[...]
    refs[-1][...] = (0.5 * total + other_ref[...]) / denom


def finish(own, got, other, occ_sum, virt_sum, first, step, out):
    rows, width = other.shape
    cols = own.shape[2]
    base = first // step
    here = pl.BlockSpec((1, rows, step), lambda j: (0, 0, j))
    there = pl.BlockSpec((rows, step), lambda j: (0, base + j))
    earlier = [] if out is None else [out]
    return pl.pallas_call(
        finish_kernel,
        grid=(cols // step,),
        in_specs=[
            here,
            here,
            there,
            pl.BlockSpec((rows, 1), lambda j: (0, 0)),
            pl.BlockSpec((1, step), lambda j: (0, base + j)),
        ]
        + [pl.BlockSpec(memory_space=pl.ANY)] * len(earlier),
        out_specs=there,
        out_shape=jax.ShapeDtypeStruct((rows, width), F32),
        input_output_aliases={5: 0} if earlier else {},
        compiler_params=params(),
        cost_estimate=cost(0, 0),
        name="finish_rows",
    )(own, got, other, occ_sum, virt_sum, *earlier)


def ranks(named, experts):
    blocks, top, rows = named.shape
    flat = named.reshape(blocks, top * rows)
    onehot = flat[:, :, None] == jnp.arange(experts, dtype=jnp.int32)
    before = jnp.tri(top * rows, k=-1, dtype=BF16)
    count = jnp.einsum("ij,bje->bie", before, onehot.astype(BF16), preferred_element_type=F32)
    shape = (blocks, top, rows, experts)
    return onehot.reshape(shape), count.astype(jnp.int32).reshape(shape)


def per_device(
    amplitudes, screen, integrals, other, occ_first, occ_second, virt_first, virt_second
):
    rows, top, width = amplitudes.shape
    n_pair = lax.axis_size("pair")
    n_virt = lax.axis_size("virt")
    cd_dev, _, cols = integrals.shape
    experts = cd_dev * n_pair
    cap = rows * top * 2 // experts
    quarter = width // n_virt
    pair = lax.axis_index("pair")
    virt = lax.axis_index("virt")
    groups = n_pair // 2
    place = virt.astype(jnp.int32).reshape(1)
    block = cd_dev * cap

    def hop(x, bits):
        return lax.ppermute(x, "pair", [(i, i ^ bits) for i in range(n_pair)])

    def swap(x, bits):
        return lax.ppermute(x, "virt", [(i, i ^ bits) for i in range(n_virt)])

    named = screen.T
    onehot, rank = ranks(named[None], experts)
    slot = jnp.sum(jnp.where(onehot, rank, 0), axis=3)[0]
    partner = lax.bitwise_xor(named // cd_dev, pair.astype(jnp.int32))
    codes = partner * block + named % cd_dev * cap + slot
    tiles = lax.dynamic_slice_in_dim(amplitudes, virt * quarter, quarter, 2)
    tiles = tiles.transpose(1, 0, 2)
    packed = pack(codes, tiles, n_pair, block)

    early = [k for k in range(n_pair) if k // 2 % 2]
    late = [k for k in range(1, n_pair) if not k // 2 % 2]
    far = [k for ks in (early, late) for k in ks if k >= n_pair // 2]
    close = [k for ks in (early, late) for k in ks if k < n_pair // 2]
    held = {k: {0: x} for k, x in enumerate(packed)}
    shared = []

    def share(k, *waits):
        bits = n_virt // 2
        while bits > 1:
            more = {at | bits: swap(after(x, *waits), bits) for at, x in held[k].items()}
            held[k].update(more)
            bits //= 2
        shared.append(list(held[k].values())[-1])

    def send(ks, n):
        if n < len(ks):
            waits = [held[ks[n - 1]][0]] if n else []
            held[ks[n]] = {0: hop(after(packed[ks[n]], *waits), ks[n])}
            return [held[ks[n]][0]]
        return []

    share(0)
    for n in range(len(far) - 1):
        under_way = send(far, n) + send(close, n) + shared[-1:]
        if n:
            share(close[n - 1])
            share(far[n - 1])
            under_way += shared[-2:]
        if n == 1:
            at = after(named, held[close[0]][0])
            owners = [named] + [hop(at, 2 * r) for r in range(1, groups)]
            under_way += owners[1:]
        place = pin(place, *under_way)
    shares = [0] + [k for both in zip(far, close) for k in both] + far[-1:]

    all_hot, all_rank = ranks(jnp.stack(owners), experts)
    inv = jnp.sum(jnp.where(all_hot, all_rank + 1, 0), axis=1) - 1
    mine = lax.dynamic_slice_in_dim(inv, pair * cd_dev, cd_dev, 2)
    theirs = lax.dynamic_slice_in_dim(inv, lax.bitwise_xor(pair, 1) * cd_dev, cd_dev, 2)
    inv = jnp.concatenate([mine, theirs], axis=2)

    unit = cols // sum(CHUNKS)
    spans = [(unit * sum(CHUNKS[:j]), unit * size) for j, size in enumerate(CHUNKS)]
    count = len(spans)
    cuts, near_of = [], []
    for j, ((first, size), n) in enumerate(zip(spans, SPLIT)):
        cuts += [(first + i * size // n, size // n) for i in range(n)]
        near_of += [(j, i) for i in range(n)]
    levels = groups.bit_length() - 1
    made, moved, near, state = {}, {}, {}, {}
    done = []

    def make(pieces, span, key, *waits, flops=HEAVY):
        at = after(place, *done[-1:], *waits)
        kept, sent = product(at, pieces, integrals, *span, cap, flops)
        made[key], moved[key] = kept, hop(sent, 1)
        done.append(kept)

    def first_rows(j, *waits):
        sent = merge(after(place, *done[-1:], *waits), inv, made["early", j], moved["early", j], None)
        near[j] = hop(sent, 2)
        done.append(sent)

    def second_rows(j, *waits):
        at = after(place, *done[-1:], *waits)
        kept, sent = merge(at, inv, made["late", j], moved["late", j], near[near_of[j][0]], near_of[j][1], HEAVY if j >= HM else 0)
        state[j] = (kept, hop(sent, 4))
        done.append(kept)

    def more_rows(j, level):
        kept, sent = halve(after(state[j][0], *done[-1:]), state[j][1])
        state[j] = (kept, hop(sent, 2 << level))
        done.append(kept)

    rows_early = [k for k in shares if k in early]
    rows_late = [k for k in shares if k not in early]

    def gather(ks, joined, *waits):
        pieces = []
        for ks in [ks] if joined else [[k] for k in ks]:
            for at in held[ks[0]]:
                x = jnp.concatenate([held[k][at] for k in ks])
                if at and ks[-1] == far[-1]:
                    x = after(x, *waits)
                for bit, y in ((0, x), (1, swap(x, 1))):
                    pieces.append((y.reshape(len(ks), cd_dev, cap, quarter), at | bit, tuple(ks)))
        return pieces

    last = len(far) - 1
    send(far, last)
    share(close[last - 1])
    share(far[last - 1])
    pieces = gather(rows_early, EARLY_JOINED)
    make(pieces, spans[0], ("early", 0))
    waits = [held[far[last]][0], *shared[-2:]]
    for j in range(1, count):
        make(pieces, spans[j], ("early", j), *waits)
        if j == 1:
            share(far[last])
        waits = shared[-1:]
        first_rows(j - 1)
    pieces = gather(rows_late, False, made["early", 1])
    make(pieces, cuts[0], ("late", 0))
    make(pieces, cuts[1], ("late", 1), flops=SECOND)
    first_rows(count - 1)
    for j in range(len(cuts)):
        second_rows(j, *[state[i][1] for i in GATES.get(("M", j), ())])
        if j + 2 < len(cuts):
            make(pieces, cuts[j + 2], ("late", j + 2), *[state[i][1] for i in GATES.get(("P", j + 2), ())])
    for level in range(2, levels):
        for j in range(len(cuts)):
            more_rows(j, level)

    tile = virt_first.shape[1]
    tile_sq = tile * tile
    start_col = virt * cols
    tile_pair = start_col // tile_sq
    first_a = start_col % tile_sq // tile
    energy_a = lax.dynamic_slice(virt_first, (tile_pair, first_a), (1, cols // tile)).reshape(-1)
    energy_b = lax.dynamic_slice_in_dim(virt_second, tile_pair, 1, 0).reshape(-1)
    virt_sum = (energy_a[:, None] + energy_b[None, :]).reshape(1, cols)
    per_i = occ_second.shape[0]
    energy_i = lax.dynamic_slice_in_dim(occ_first, pair * (rows // per_i), rows // per_i, 0)
    occ_sum = (energy_i[:, None] + occ_second[None, :]).reshape(rows, 1)
    out = None
    for j, (first, size) in enumerate(cuts):
        own = after(state[j][0], *done[-1:])
        out = finish(own, state[j][1], other, occ_sum, virt_sum, first, size // 2, out)
    return out


def solution(mesh):
    return jax.shard_map(
        per_device,
        mesh=mesh,
        in_specs=(
            P("pair", None, None),
            P("pair", None),
            P("pair", None, "virt"),
            P("pair", "virt"),
            P(),
            P(),
            P(),
            P(),
        ),
        out_specs=P("pair", "virt"),
        check_vma=False,
    )
```

```python
import functools
import math

import jax
import jax.numpy as jnp
from jax import lax
from jax.experimental import pallas as pl
from jax.experimental.pallas import tpu as pltpu
from jax.sharding import PartitionSpec as P

MIB = 1024 * 1024
F32 = jnp.float32
BF16 = jnp.bfloat16
CHUNKS = (4, 4)
SPLIT = (2, 2)
GATES = {("M", 2): (0,)}
HM = 2
HEAVY = 1e11
EARLY_JOINED = True
MAX_STEP = 512
SECOND = 8e9


def params(mib=16):
    return pltpu.CompilerParams(vmem_limit_bytes=mib * MIB)


def cost(flops, nbytes):
    return pl.CostEstimate(flops=int(flops), bytes_accessed=int(nbytes), transcendentals=0)


def encode(v):
    w = v * 8.0
    sq = w * w
    quad = sq * sq
    return ((w * jnp.abs(w)) * (quad * sq)).astype(BF16)


def decode(code):
    c = code.astype(F32)
    a = jnp.abs(c)
    t = lax.rsqrt(jnp.maximum(a, 1e-37))
    u = lax.rsqrt(t)
    root = u * lax.rsqrt(u) * 0.125
    root = jnp.where(a < 1e-37, 0.0, root)
    return jnp.where(c < 0.0, -root, root)


def after(x, *earlier):
    earlier = [y for y in earlier if y is not None]
    return lax.optimization_barrier((x, *earlier))[0] if earlier else x


def pin_kernel(place_ref, out_ref):
    out_ref[0] = place_ref[0]


def pin(place, *earlier):
    scalar = pl.BlockSpec(memory_space=pltpu.SMEM)
    return pl.pallas_call(
        pin_kernel,
        in_specs=[scalar],
        out_specs=scalar,
        out_shape=jax.ShapeDtypeStruct((1,), jnp.int32),
        cost_estimate=cost(HEAVY, 8),
        name="pin",
    )(after(place, *earlier))


def pack_kernel(codes_ref, tiles_ref, *outs):
    top, rows, _ = tiles_ref.shape
    block = outs[0].shape[0]
    lane = lax.broadcasted_iota(jnp.int32, (block, rows), 0)
    for at, out in enumerate(outs):
        total = None
        for k in range(top):
            pick = (lane == codes_ref[k : k + 1, :] - at * block).astype(F32).astype(BF16)
            part = jnp.dot(pick, tiles_ref[k], preferred_element_type=F32)
            total = part if total is None else total + part
        out[...] = total.astype(BF16)


def pack(codes, tiles, count, block):
    top, rows, width = tiles.shape
    n_slots = count * block
    return pl.pallas_call(
        pack_kernel,
        out_shape=[jax.ShapeDtypeStruct((block, width), BF16)] * count,
        compiler_params=params(),
        cost_estimate=cost(0, 0),
        name="pack_tiles",
    )(codes, tiles)


def product_kernel(layout, place_ref, *refs):
    *parts, w_ref, keep_ref, send_ref = refs
    cap = keep_ref.shape[2]
    sides = {}
    for part, (rel, ks) in zip(parts, layout):
        sides.setdefault(rel, []).append((part, ks))
    total = None
    for rel, blocks in sides.items():
        lhs = [part[:, 0].reshape(-1, part.shape[3]) for part, _ in blocks]
        lhs = jnp.concatenate(lhs, axis=0) if len(lhs) > 1 else lhs[0]
        size = lhs.shape[1]
        start = pl.multiple_of(lax.bitwise_xor(place_ref[0], rel) * size, size)
        more = jnp.dot(lhs, w_ref[0, pl.ds(start, size), :], preferred_element_type=F32)
        total = more if total is None else total + more
    for n, k in enumerate([k for _, ks in sides[0] for k in ks]):
        block = total[n * cap : (n + 1) * cap]
        if k % 2:
            send_ref[0, k // 4] = encode(block)
        else:
            keep_ref[0, k // 4] = block


def product(place, pieces, integrals, first, cols, cap, flops):
    lhs = [piece[0] for piece in pieces]
    layout = tuple(piece[1:] for piece in pieces)
    experts, width, _ = integrals.shape
    half = sum(x.shape[0] for x, rel, _ in pieces if rel == 0) // 2
    step = math.gcd(first, cols, MAX_STEP)
    base, steps = first // step, cols // step
    out = pl.BlockSpec((1, half, cap, step), lambda t, s: (t // steps, 0, 0, t % steps))
    shape = (experts, half, cap, cols)
    return pl.pallas_call(
        functools.partial(product_kernel, layout),
        grid_spec=pltpu.PrefetchScalarGridSpec(
            num_scalar_prefetch=1,
            grid=(experts * steps,),
            in_specs=[
                pl.BlockSpec((x.shape[0], 1, *x.shape[2:]), lambda t, s: (0, t // steps, 0, 0))
                for x in lhs
            ]
            + [pl.BlockSpec((1, width, step), lambda t, s: (t // steps, 0, base + t % steps))],
            out_specs=[out, out],
        ),
        out_shape=[jax.ShapeDtypeStruct(shape, F32), jax.ShapeDtypeStruct(shape, BF16)],
        compiler_params=params(36),
        cost_estimate=cost(flops, 0),
        name="tile_products",
    )(place, *lhs, integrals)


def placement(inv, cap):
    lane = jnp.arange(4 * cap, dtype=jnp.int32)
    hit = None
    for c in range(4):
        slot = inv[:, :, c : c + 1]
        one = lane == jnp.where(slot < 0, -1, slot + c * cap)
        hit = one if hit is None else hit | one
    return hit.astype(BF16)


def dense_rows(pick, values):
    high = values.astype(BF16)
    low = (values - high.astype(F32)).astype(BF16)
    dense = jnp.dot(pick, high, preferred_element_type=F32)
    return dense + jnp.dot(pick, low, preferred_element_type=F32)


def merge_kernel(place_ref, pick_ref, keep0, keep1, got0, got1, *refs):
    values = [keep0[0, 0], keep1[0, 0], decode(got0[0, 0]), decode(got1[0, 0])]
    dense = dense_rows(pick_ref[0], jnp.concatenate(values, axis=0))
    if len(refs) == 1:
        refs[0][0] = encode(dense)
        return
    near_ref, kept_ref, send_ref = refs
    dense = dense + decode(near_ref[0])

    @pl.when(pl.program_id(0) % 2 == 0)
    def _():
        kept_ref[0] = dense

    @pl.when(pl.program_id(0) % 2 == 1)
    def _():
        send_ref[0] = encode(dense)


def merge(place, pick, keep, got, near, at=0, flops=0):
    _, half, cap, cols = keep.shape
    rows = pick.shape[1]
    odd = near is None

    def spec(c):
        return pl.BlockSpec((1, 1, cap, cols), lambda i, s: (c, i, 0, 0))

    each = pl.BlockSpec((1, rows, cols), lambda i, s: (i, 0, 0))
    second = pl.BlockSpec((1, rows, cols), lambda i, s: (i // 2, 0, 0))
    shape = functools.partial(jax.ShapeDtypeStruct, (half // 2, rows, cols))
    return pl.pallas_call(
        merge_kernel,
        grid_spec=pltpu.PrefetchScalarGridSpec(
            num_scalar_prefetch=1,
            grid=(half,),
            in_specs=[pl.BlockSpec((1, rows, 4 * cap), lambda i, s: (2 * i + odd, 0, 0))]
            + [spec(0), spec(1)] * 2
            + [pl.BlockSpec((1, rows, cols), lambda i, s: (i, 0, at))] * (not odd),
            out_specs=each if odd else [second, second],
        ),
        out_shape=jax.ShapeDtypeStruct((half, rows, cols), BF16) if odd else [shape(F32), shape(BF16)],
        compiler_params=params(),
        cost_estimate=cost(flops, 0),
        name="merge_rows",
    )(place, pick, keep, keep, got, got, *([] if odd else [near]))


def halve_kernel(kept_ref, got_ref, out_ref, send_ref):
    out_ref[0] = kept_ref[0] + decode(got_ref[0])
    send_ref[0] = encode(kept_ref[1] + decode(got_ref[1]))


def halve(kept, got):
    count, rows, cols = kept.shape
    step = rows // 2
    two = pl.BlockSpec((2, step, cols), lambda i, r: (i, r, 0))
    one = pl.BlockSpec((1, step, cols), lambda i, r: (i, r, 0))
    shape = (count // 2, rows, cols)
    return pl.pallas_call(
        halve_kernel,
        grid=(count // 2, rows // step),
        in_specs=[two, two],
        out_specs=[one, one],
        out_shape=[jax.ShapeDtypeStruct(shape, F32), jax.ShapeDtypeStruct(shape, BF16)],
        compiler_params=params(),
        cost_estimate=cost(0, 0),
        name="halve_rows",
    )(kept, got)


def finish_kernel(own_ref, got_ref, other_ref, occ_ref, virt_ref, *refs):
    total = own_ref[0] + decode(got_ref[0])
    denom = occ_ref[...] - virt_ref[...]
    refs[-1][...] = (0.5 * total + other_ref[...]) / denom


def finish(own, got, other, occ_sum, virt_sum, first, step, out):
    rows, width = other.shape
    cols = own.shape[2]
    base = first // step
    here = pl.BlockSpec((1, rows, step), lambda j: (0, 0, j))
    there = pl.BlockSpec((rows, step), lambda j: (0, base + j))
    earlier = [] if out is None else [out]
    return pl.pallas_call(
        finish_kernel,
        grid=(cols // step,),
        in_specs=[
            here,
            here,
            there,
            pl.BlockSpec((rows, 1), lambda j: (0, 0)),
            pl.BlockSpec((1, step), lambda j: (0, base + j)),
        ]
        + [pl.BlockSpec(memory_space=pl.ANY)] * len(earlier),
        out_specs=there,
        out_shape=jax.ShapeDtypeStruct((rows, width), F32),
        input_output_aliases={5: 0} if earlier else {},
        compiler_params=params(),
        cost_estimate=cost(0, 0),
        name="finish_rows",
    )(own, got, other, occ_sum, virt_sum, *earlier)


def ranks(named, experts):
    blocks, top, rows = named.shape
    flat = named.reshape(blocks, top * rows)
    onehot = flat[:, :, None] == jnp.arange(experts, dtype=jnp.int32)
    before = jnp.tri(top * rows, k=-1, dtype=BF16)
    count = jnp.einsum("ij,bje->bie", before, onehot.astype(BF16), preferred_element_type=F32)
    shape = (blocks, top, rows, experts)
    return onehot.reshape(shape), count.astype(jnp.int32).reshape(shape)


def per_device(
    amplitudes, screen, integrals, other, occ_first, occ_second, virt_first, virt_second
):
    rows, top, width = amplitudes.shape
    n_pair = lax.axis_size("pair")
    n_virt = lax.axis_size("virt")
    cd_dev, _, cols = integrals.shape
    experts = cd_dev * n_pair
    cap = rows * top * 2 // experts
    quarter = width // n_virt
    pair = lax.axis_index("pair")
    virt = lax.axis_index("virt")
    groups = n_pair // 2
    place = virt.astype(jnp.int32).reshape(1)
    block = cd_dev * cap

    def hop(x, bits):
        return lax.ppermute(x, "pair", [(i, i ^ bits) for i in range(n_pair)])

    def swap(x, bits):
        return lax.ppermute(x, "virt", [(i, i ^ bits) for i in range(n_virt)])

    named = screen.T
    onehot, rank = ranks(named[None], experts)
    slot = jnp.sum(jnp.where(onehot, rank, 0), axis=3)[0]
    partner = lax.bitwise_xor(named // cd_dev, pair.astype(jnp.int32))
    codes = partner * block + named % cd_dev * cap + slot
    tiles = lax.dynamic_slice_in_dim(amplitudes, virt * quarter, quarter, 2)
    tiles = tiles.transpose(1, 0, 2)
    packed = pack(codes, tiles, n_pair, block)

    early = [k for k in range(n_pair) if k // 2 % 2]
    late = [k for k in range(1, n_pair) if not k // 2 % 2]
    far = [k for ks in (early, late) for k in ks if k >= n_pair // 2]
    close = [k for ks in (early, late) for k in ks if k < n_pair // 2]
    held = {k: {0: x} for k, x in enumerate(packed)}
    shared = []

    def share(k, *waits):
        bits = n_virt // 2
        while bits > 1:
            more = {at | bits: swap(after(x, *waits), bits) for at, x in held[k].items()}
            held[k].update(more)
            bits //= 2
        shared.append(list(held[k].values())[-1])

    def send(ks, n):
        if n < len(ks):
            waits = [held[ks[n - 1]][0]] if n else []
            held[ks[n]] = {0: hop(after(packed[ks[n]], *waits), ks[n])}
            return [held[ks[n]][0]]
        return []

    share(0)
    for n in range(len(far) - 1):
        under_way = send(far, n) + send(close, n) + shared[-1:]
        if n:
            share(close[n - 1])
            share(far[n - 1])
            under_way += shared[-2:]
        if n == 1:
            at = after(named, held[close[0]][0])
            owners = [named] + [hop(at, 2 * r) for r in range(1, groups)]
            under_way += owners[1:]
        place = pin(place, *under_way)
    shares = [0] + [k for both in zip(far, close) for k in both] + far[-1:]

    all_hot, all_rank = ranks(jnp.stack(owners), experts)
    inv = jnp.sum(jnp.where(all_hot, all_rank + 1, 0), axis=1) - 1
    mine = lax.dynamic_slice_in_dim(inv, pair * cd_dev, cd_dev, 2)
    theirs = lax.dynamic_slice_in_dim(inv, lax.bitwise_xor(pair, 1) * cd_dev, cd_dev, 2)
    inv = placement(jnp.concatenate([mine, theirs], axis=2), cap)

    unit = cols // sum(CHUNKS)
    spans = [(unit * sum(CHUNKS[:j]), unit * size) for j, size in enumerate(CHUNKS)]
    count = len(spans)
    cuts, near_of = [], []
    for j, ((first, size), n) in enumerate(zip(spans, SPLIT)):
        cuts += [(first + i * size // n, size // n) for i in range(n)]
        near_of += [(j, i) for i in range(n)]
    levels = groups.bit_length() - 1
    made, moved, near, state = {}, {}, {}, {}
    done = []

    def make(pieces, span, key, *waits, flops=HEAVY):
        at = after(place, *done[-1:], *waits)
        kept, sent = product(at, pieces, integrals, *span, cap, flops)
        made[key], moved[key] = kept, hop(sent, 1)
        done.append(kept)

    def first_rows(j, *waits):
        sent = merge(after(place, *done[-1:], *waits), inv, made["early", j], moved["early", j], None)
        near[j] = hop(sent, 2)
        done.append(sent)

    def second_rows(j, *waits):
        at = after(place, *done[-1:], *waits)
        kept, sent = merge(at, inv, made["late", j], moved["late", j], near[near_of[j][0]], near_of[j][1], HEAVY if j >= HM else 0)
        state[j] = (kept, hop(sent, 4))
        done.append(kept)

    def more_rows(j, level):
        kept, sent = halve(after(state[j][0], *done[-1:]), state[j][1])
        state[j] = (kept, hop(sent, 2 << level))
        done.append(kept)

    rows_early = [k for k in shares if k in early]
    rows_late = [k for k in shares if k not in early]

    def gather(ks, joined, *waits):
        pieces = []
        for ks in [ks] if joined else [[k] for k in ks]:
            for at in held[ks[0]]:
                x = jnp.concatenate([held[k][at] for k in ks])
                if at and ks[-1] == far[-1]:
                    x = after(x, *waits)
                for bit, y in ((0, x), (1, swap(x, 1))):
                    pieces.append((y.reshape(len(ks), cd_dev, cap, quarter), at | bit, tuple(ks)))
        return pieces

    last = len(far) - 1
    send(far, last)
    share(close[last - 1])
    share(far[last - 1])
    pieces = gather(rows_early, EARLY_JOINED)
    make(pieces, spans[0], ("early", 0))
    waits = [held[far[last]][0], *shared[-2:]]
    for j in range(1, count):
        make(pieces, spans[j], ("early", j), *waits)
        if j == 1:
            share(far[last])
        waits = shared[-1:]
        first_rows(j - 1)
    pieces = gather(rows_late, False, made["early", 1])
    make(pieces, cuts[0], ("late", 0))
    make(pieces, cuts[1], ("late", 1), flops=SECOND)
    first_rows(count - 1)
    for j in range(len(cuts)):
        second_rows(j, *[state[i][1] for i in GATES.get(("M", j), ())])
        if j + 2 < len(cuts):
            make(pieces, cuts[j + 2], ("late", j + 2), *[state[i][1] for i in GATES.get(("P", j + 2), ())])
    for level in range(2, levels):
        for j in range(len(cuts)):
            more_rows(j, level)

    tile = virt_first.shape[1]
    tile_sq = tile * tile
    start_col = virt * cols
    tile_pair = start_col // tile_sq
    first_a = start_col % tile_sq // tile
    energy_a = lax.dynamic_slice(virt_first, (tile_pair, first_a), (1, cols // tile)).reshape(-1)
    energy_b = lax.dynamic_slice_in_dim(virt_second, tile_pair, 1, 0).reshape(-1)
    virt_sum = (energy_a[:, None] + energy_b[None, :]).reshape(1, cols)
    per_i = occ_second.shape[0]
    energy_i = lax.dynamic_slice_in_dim(occ_first, pair * (rows // per_i), rows // per_i, 0)
    occ_sum = (energy_i[:, None] + occ_second[None, :]).reshape(rows, 1)
    out = None
    for j, (first, size) in enumerate(cuts):
        own = after(state[j][0], *done[-1:])
        out = finish(own, state[j][1], other, occ_sum, virt_sum, first, size // 2, out)
    return out


def solution(mesh):
    return jax.shard_map(
        per_device,
        mesh=mesh,
        in_specs=(
            P("pair", None, None),
            P("pair", None),
            P("pair", None, "virt"),
            P("pair", "virt"),
            P(),
            P(),
            P(),
            P(),
        ),
        out_specs=P("pair", "virt"),
        check_vma=False,
    )
```
